256 devices in a mesh: dp: 16 (over x, y), expert: 16 (over z, core).
Axes of the slice: x: 4, y: 4, z: 8, core: 2. Of those that a mesh axis runs over, the one named last changes fastest.
Arguments:
- tokens: bfloat16 [32768, 2048], P(('dp', 'expert')), may hold values from -6 to 6
- expert_ids: int32 [32768, 8], P(('dp', 'expert')), may hold values from 0 to 15, as said below
- gate_weights: bfloat16 [32768, 8], P(('dp', 'expert')), may hold values from 0.049804688 to 1
- w_in: bfloat16 [16, 2048, 1536], P('expert'), may hold values from -0.125 to 0.125
- w_in_scale: float32 [16, 16, 12], P('expert'), may hold values from 0.3 to 3
- w_out: bfloat16 [16, 768, 2048], P('expert'), may hold values from -0.21875 to 0.21875
- w_out_scale: float32 [16, 6, 16], P('expert'), may hold values from 0.3 to 3
Outputs:
- mixed: bfloat16 [32768, 2048], P(('dp', 'expert'))
The draws below stay inside these ranges and needn't reach their ends.
Inputs may be any that keep to these rules, and one draw needn't show every extreme that they name: `expert_ids`: each token names 8 different experts. In every block of 128 rows, each expert is named by exactly 96, 80, 48 or 32 rows, a quarter of the experts at each count, so at most 96 rows of one device name one expert; the counts are the same in all blocks of one block of 2048 rows, and which experts take which count is drawn for each such group.
All inputs are finite; a program needn't handle non-finite values.
Results may differ from the reference program's by a relative error of at most 0.015.
Values may be sent and summed in bfloat16 or wider, within the bound.
No kernel may reach another device: no remote copies, remote signals or barrier semaphores. Data moves between devices by JAX's collectives and lax.ppermute only.
A program may use at most 128 MiB of HBM per device.

```python
import math
import jax
import jax.numpy as jnp
from jax import lax

D = 2048
F = 768
EXPERTS = 16
TOPK = 8
QB = 128
TOK_DEV = 128
MOST = 96
GROUP_TOK = 2048
TOKENS = 32768
N_DP = 16
N_EXPERT = 16


def draw_expert_ids(key, part):
    key = jax.random.fold_in(key, 7)
    mean_load = TOK_DEV * TOPK // EXPERTS
    quarter = EXPERTS // 4
    levels = jnp.array([3 * mean_load // 2, 5 * mean_load // 4, 3 * mean_load // 4, mean_load // 2], jnp.int32)
    by_rank = levels[jnp.arange(EXPERTS) // quarter]
    groups = TOKENS // GROUP_TOK
    members = GROUP_TOK // TOK_DEV
    group_keys = jax.random.split(jax.random.fold_in(key, 1), groups)

    def group_counts(group_key):
        ranking = jax.random.permutation(group_key, EXPERTS)
        return jnp.zeros((EXPERTS,), jnp.int32).at[ranking].set(by_rank)
    counts = jax.vmap(group_counts)(group_keys)
    device_counts = jnp.repeat(counts, members, axis=0)
    device_keys = jax.random.split(jax.random.fold_in(key, 2), groups * members)

    def device_ids(device_key, device_count):
        listing = jnp.repeat(jnp.arange(EXPERTS, dtype=jnp.int32), device_count, total_repeat_length=TOK_DEV * TOPK)
        layout = listing.reshape(TOPK, TOK_DEV).T
        perm_key, turn_key = jax.random.split(device_key)
        shuffled = layout[jax.random.permutation(perm_key, TOK_DEV)]
        rotation = jax.random.randint(turn_key, (TOK_DEV, 1), 0, TOPK)
        column = (jnp.arange(TOPK)[None, :] + rotation) % TOPK
        return jnp.take_along_axis(shuffled, column, axis=1)
    chosen = jax.vmap(device_ids)(device_keys, device_counts)
    return chosen.reshape(TOKENS, TOPK).astype(jnp.int32)


def block_levels(key, dims, shards, smallest, high):
    loudness, own = 1.0, jax.random.fold_in(key, 6)
    for position, blocks in shards:
        heights = jnp.exp(jax.random.uniform(jax.random.fold_in(own, position), (blocks,), jnp.float32, smallest / len(shards), high / len(shards)))
        loudness = loudness * jnp.repeat(heights, dims[position] // blocks).reshape([-1 if axis == position else 1 for axis in range(len(dims))])
    return loudness


def normal_values(own_key, shape, spread, most, cuts=(), held_as=jnp.bfloat16):
    result = spread * jax.random.normal(own_key, shape, jnp.float32)
    if cuts:
        result = result * block_levels(own_key, shape, cuts, -0.22, 0.18)
    return jnp.clip(result, -most, most).astype(held_as)


def setup_inputs(seed: int = 0) -> dict:
    keys = jax.random.split(jax.random.key(seed), 8)
    tokens = normal_values(keys[0], (TOKENS, D), 1.0, 6.0, ((0, 256),))
    expert_ids = draw_expert_ids(jax.random.fold_in(keys[7], 71), 0)
    gate_weights = jnp.clip(jnp.exp(math.log(1.0) - 2.9996462 * jax.random.uniform(keys[2], (TOKENS, TOPK), jnp.float32) ** block_levels(keys[2], (TOKENS, TOPK), ((0, 256),), -0.2, 0.2)), 0.049804688, 1.0).astype(jnp.bfloat16)
    w_in = normal_values(keys[3], (EXPERTS, D, 2 * F), D ** -0.5, 0.125, ((0, 16),))
    w_in_scale = jnp.clip(jnp.exp(math.log(3.0) - 2.3025851 * jax.random.uniform(keys[4], (EXPERTS, D // QB, 2 * F // QB), jnp.float32) ** block_levels(keys[4], (EXPERTS, D // QB, 2 * F // QB), ((0, 16),), -0.2, 0.2)), 0.3, 3.0)
    w_out = normal_values(keys[5], (EXPERTS, F, D), F ** -0.5, 0.21875, ((0, 16),))
    w_out_scale = jnp.clip(jnp.exp(math.log(3.0) - 2.3025851 * jax.random.uniform(keys[6], (EXPERTS, F // QB, D // QB), jnp.float32) ** block_levels(keys[6], (EXPERTS, F // QB, D // QB), ((0, 16),), -0.2, 0.2)), 0.3, 3.0)
    return dict(tokens=tokens, expert_ids=expert_ids, gate_weights=gate_weights, w_in=w_in, w_in_scale=w_in_scale, w_out=w_out, w_out_scale=w_out_scale)


def dequantize(weight, scales):
    expanded = jnp.repeat(jnp.repeat(scales, QB, axis=0), QB, axis=1)
    return (weight.astype(jnp.float32) * expanded).astype(jnp.bfloat16)


def reference(tokens, expert_ids, gate_weights, w_in, w_in_scale, w_out, w_out_scale):
    token_total = tokens.shape[0]
    block_rows = N_EXPERT * MOST
    capacity = N_DP * block_rows
    gate_values = gate_weights.astype(jnp.float32)
    half_width = w_out.shape[1]

    def per_expert(expert, totals):
        matches = expert_ids == expert
        member = jnp.any(matches, axis=1)
        gate_sum = jnp.sum(jnp.where(matches, gate_values, 0.0), axis=1)
        running = (jnp.cumsum(member.astype(jnp.int32)) - 1).astype(jnp.int32)
        slot_at = jnp.where(member, running, capacity).astype(jnp.int32)
        source = jnp.zeros((capacity,), jnp.int32).at[slot_at].set(jnp.arange(token_total, dtype=jnp.int32), mode="drop")
        filled = jnp.arange(capacity) < jnp.sum(member.astype(jnp.int32))
        deq_in = dequantize(w_in[expert], w_in_scale[expert])
        deq_out = dequantize(w_out[expert], w_out_scale[expert])

        def per_block(block_index):
            row_at = (block_index * block_rows).astype(jnp.int32)
            indices = lax.dynamic_slice_in_dim(source, row_at, block_rows, 0)
            kept_rows = lax.dynamic_slice_in_dim(filled, row_at, block_rows, 0)
            row_block = tokens[indices]
            gate_block = jnp.where(kept_rows, gate_sum[indices], 0.0)
            both_parts = jnp.dot(row_block, deq_in, preferred_element_type=jnp.float32)
            hidden = (jax.nn.silu(both_parts[:, :half_width]) * both_parts[:, half_width:]).astype(jnp.bfloat16)
            outcome = jnp.dot(hidden, deq_out, preferred_element_type=jnp.float32)
            return (gate_block[:, None] * outcome).astype(jnp.bfloat16)

        expert_terms = lax.map(per_block, jnp.arange(N_DP, dtype=jnp.int32)).reshape(capacity, tokens.shape[1])
        contrib = jnp.where(filled[:, None], expert_terms.astype(jnp.float32), 0.0)
        return totals.at[source].add(contrib)

    totals = lax.fori_loop(0, EXPERTS, per_expert, jnp.zeros(tokens.shape, jnp.float32))
    return totals.astype(jnp.bfloat16)
```

```python
import jax
import jax.numpy as jnp
from jax import lax
from jax.sharding import PartitionSpec as P

QB = 128
CORES = 2


def dequantize(weight, scales):
    rows, cols = weight.shape
    blocks = weight.astype(jnp.float32).reshape(rows // QB, QB, cols // QB, QB)
    return (blocks * scales[:, None, :, None]).reshape(rows, cols).astype(jnp.bfloat16)


def expert(rows, gates, deq_in, deq_out):
    half = deq_out.shape[0]
    both = jnp.dot(rows, deq_in, preferred_element_type=jnp.float32)
    hidden = (jax.nn.silu(both[:, :half]) * both[:, half:] * gates[:, None]).astype(jnp.bfloat16)
    return jnp.dot(hidden, deq_out, preferred_element_type=jnp.float32)


def body(tokens, expert_ids, gate_weights, w_in, w_in_scale, w_out, w_out_scale):
    devices = lax.axis_size("expert")
    chips = devices // CORES
    far = chips // 2
    here = lax.axis_index("expert")
    chip, core = here // CORES, here % CORES
    count = tokens.shape[0]
    cut = count // 2

    def hop(value, step):
        pairs = [
            (z * CORES + c, ((z + step) % chips) * CORES + c)
            for z in range(chips)
            for c in range(CORES)
        ]
        return lax.ppermute(value, "expert", pairs)

    def swap(value):
        pairs = [(d, d ^ 1) for d in range(devices)]
        return lax.ppermute(value, "expert", pairs)

    first, second = tokens[:cut], tokens[cut:]
    up = {0: (first, second)}
    down = {0: (first, second)}
    for s in range(1, far):
        up[s] = tuple(hop(v, 1) for v in up[s - 1])
        down[s] = tuple(hop(v, -1) for v in down[s - 1])
    last = (hop(up[far - 1][0], 1), hop(down[far - 1][1], -1))

    own_in, own_out = dequantize(w_in[0], w_in_scale[0]), dequantize(w_out[0], w_out_scale[0])
    sib_in, sib_out = swap(own_in), swap(own_out)

    ids = jnp.arange(devices, dtype=jnp.int32)
    matches = expert_ids[:, :, None] == ids[None, None, :]
    dense = jnp.sum(jnp.where(matches, gate_weights[:, :, None].astype(jnp.float32), 0.0), axis=1)
    groups = [[z * CORES + c for z in range(chips)] for c in range(CORES)]
    spread = lax.all_gather(
        dense.T.astype(jnp.bfloat16), "expert", axis=0, tiled=False, axis_index_groups=groups
    )
    spread = jnp.concatenate([spread, spread], axis=0)
    spread = lax.dynamic_slice_in_dim(spread, chip, chips, 0).astype(jnp.float32)
    gate_own = lax.dynamic_index_in_dim(spread, here, 1, keepdims=False)
    gate_sib = lax.dynamic_index_in_dim(spread, here + 1 - 2 * core, 1, keepdims=False)

    def both_experts(rows, at):
        g0 = jnp.concatenate([gate_own[k] for k in at])
        g1 = jnp.concatenate([gate_sib[k] for k in at])
        return expert(rows, g0, own_in, own_out) + expert(rows, g1, sib_in, sib_out)

    mine = both_experts(tokens, (0,))
    from_below, from_above = {}, {}
    for s in range(1, far):
        got = both_experts(jnp.concatenate([*up[s], *down[s]]), (chips - s, s))
        from_below[s], from_above[s] = got[:count], got[count:]
    farthest = both_experts(jnp.concatenate(last), (far,))

    def add(moving, local):
        return (moving.astype(jnp.float32) + local).astype(jnp.bfloat16)

    rise = [hop(farthest[:cut].astype(jnp.bfloat16), 1), None]
    fall = [None, hop(farthest[cut:].astype(jnp.bfloat16), -1)]
    for s in range(far - 1, 0, -1):
        above = (from_above[s][:cut], from_above[s][cut:])
        below = (from_below[s][:cut], from_below[s][cut:])
        rise = [
            hop(loc.astype(jnp.bfloat16) if mov is None else add(mov, loc), 1)
            for mov, loc in zip(rise, above)
        ]
        fall = [
            hop(loc.astype(jnp.bfloat16) if mov is None else add(mov, loc), -1)
            for mov, loc in zip(fall, below)
        ]
    total = mine + jnp.concatenate(rise).astype(jnp.float32) + jnp.concatenate(fall).astype(jnp.float32)
    return total.astype(jnp.bfloat16)


def solution(mesh):
    placed = (
        P(("dp", "expert"), None),
        P(("dp", "expert"), None),
        P(("dp", "expert"), None),
        P("expert", None, None),
        P("expert", None, None),
        P("expert", None, None),
        P("expert", None, None),
    )
    return jax.shard_map(
        body, mesh=mesh, in_specs=placed, out_specs=P(("dp", "expert"), None), check_vma=False
    )
```

```python
import functools

import jax
import jax.numpy as jnp
from jax import lax
from jax.experimental import pallas as pl
from jax.experimental.pallas import tpu as pltpu
from jax.sharding import PartitionSpec as P

QB = 128
CORES = 2
LANES = 128
PIECES = 2
MIB = 1024 * 1024
VMEM_SPEC = pl.BlockSpec(memory_space=pltpu.VMEM)
SMEM_SPEC = pl.BlockSpec(memory_space=pltpu.SMEM)
ANY_SPEC = pl.BlockSpec(memory_space=pl.ANY)
QUICK = pl.CostEstimate(flops=1, bytes_accessed=1, transcendentals=0)


def in_hbm(value):
    return pltpu.with_memory_space_constraint(value, pltpu.HBM)


def in_vmem(value):
    return pltpu.with_memory_space_constraint(value, pltpu.VMEM)


def params(mib):
    return pltpu.CompilerParams(vmem_limit_bytes=int(mib * MIB))


def prepare_kernel(tokens_ref, ids_ref, gates_ref, *refs):
    outs, (ids_buf, gates_buf, sems) = refs[:PIECES], refs[PIECES:]
    count, width = tokens_ref.shape
    cut = count // PIECES
    small = [
        pltpu.make_async_copy(ids_ref, ids_buf, sems.at[PIECES]),
        pltpu.make_async_copy(gates_ref, gates_buf, sems.at[PIECES + 1]),
    ]
    large = [
        pltpu.make_async_copy(
            tokens_ref.at[pl.ds(i * cut, cut)], out.at[:, pl.ds(0, width)], sems.at[i]
        )
        for i, out in enumerate(outs)
    ]
    for copy in small + large:
        copy.start()
    for copy in small:
        copy.wait()
    ids, gates = ids_buf[...], gates_buf[...].astype(jnp.float32)
    row = lax.broadcasted_iota(jnp.int32, (LANES, count), 0)
    dense = jnp.zeros((LANES, count), jnp.float32)
    for k in range(ids.shape[0]):
        dense = dense + jnp.where(ids[k : k + 1, :] == row, gates[k : k + 1, :], 0.0)
    dense = dense.T.astype(jnp.bfloat16)
    for i, out in enumerate(outs):
        out[:, width:] = dense[i * cut : (i + 1) * cut]
    for copy in large:
        copy.wait()


def prepare(tokens, expert_ids, gate_weights):
    count, width = tokens.shape
    slots = expert_ids.shape[1]
    return pl.pallas_call(
        prepare_kernel,
        out_shape=[pltpu.VMEM((count // PIECES, width + LANES), jnp.bfloat16)] * PIECES,
        in_specs=[ANY_SPEC] * 3,
        out_specs=[VMEM_SPEC] * PIECES,
        scratch_shapes=[
            pltpu.VMEM((slots, count), jnp.int32),
            pltpu.VMEM((slots, count), jnp.bfloat16),
            pltpu.SemaphoreType.DMA((PIECES + 2,)),
        ],
        compiler_params=params(1),
        cost_estimate=QUICK,
        name="prepare",
    )(in_hbm(tokens), in_hbm(expert_ids.T), in_hbm(gate_weights.T))


def dequantize_kernel(begins, n_kept, copy_out, scale_ref, *refs):
    n, refs = len(begins), refs[n_kept:]
    weights, outs, refs = refs[:n], refs[n : 2 * n], refs[2 * n :]
    works, refs = (refs[:n], refs[n:]) if copy_out else (outs, refs)
    in_sems = refs[0]
    copies, sent = [], []
    for weight, work in zip(weights, works):
        for i in range(weight.shape[0] // QB):
            at = pl.ds(i * QB, QB)
            copies.append(
                pltpu.make_async_copy(weight.at[at], work.at[at], in_sems.at[len(copies)])
            )
            copies[-1].start()
    for begin, work, out in zip(begins, works, outs):
        rows, cols = work.shape
        for i in range(rows // QB):
            copies[len(sent)].wait()
            for j in range(cols // QB):
                at = slice(i * QB, (i + 1) * QB), slice(j * QB, (j + 1) * QB)
                scale = scale_ref[begin + i * (cols // QB) + j]
                work[at] = (work[at].astype(jnp.float32) * scale).astype(jnp.bfloat16)
            sent.append(None)
            if copy_out:
                at = pl.ds(i * QB, QB)
                sent[-1] = pltpu.make_async_copy(
                    work.at[at], out.at[at], refs[1].at[len(sent) - 1]
                )
                sent[-1].start()
    for copy in sent:
        if copy is not None:
            copy.wait()


def dequantize(weights, scales, begins, copy_out=False, kept=()):
    blocks = sum(w.shape[0] // QB for w in weights)
    space = pltpu.HBM if copy_out else pltpu.VMEM
    size = sum(w.size for w in weights) * 2 / MIB if copy_out else 0
    return pl.pallas_call(
        functools.partial(dequantize_kernel, begins, len(kept), copy_out),
        out_shape=[space(w.shape, jnp.bfloat16) for w in weights],
        in_specs=[SMEM_SPEC] + [VMEM_SPEC] * len(kept) + [ANY_SPEC] * len(weights),
        out_specs=[ANY_SPEC if copy_out else VMEM_SPEC] * len(weights),
        scratch_shapes=[pltpu.VMEM(w.shape, jnp.bfloat16) for w in weights if copy_out]
        + [pltpu.SemaphoreType.DMA((blocks,))] * (2 if copy_out else 1),
        compiler_params=params(0.5 + size),
        cost_estimate=QUICK,
        name="dequantize",
    )(scales, *(in_vmem(v) for v in kept), *(in_hbm(w) for w in weights))


def experts_kernel(n_parts, n_experts, lanes_ref, *refs):
    parts, refs = refs[:n_parts], refs[n_parts:]
    w_in, refs = refs[:n_experts], refs[n_experts:]
    w_out, refs = refs[:n_experts], refs[n_experts:]
    outs, (rows_ref, hidden_ref) = refs[:-2], refs[-2:]
    half, width = w_out[0].shape
    cut = parts[0].shape[0]
    lane = lax.broadcasted_iota(jnp.int32, (n_parts * cut, LANES), 1)
    for p, part in enumerate(parts):
        rows_ref[p * cut : (p + 1) * cut, :] = part[:, :width]
    gates = jnp.concatenate([part[:, width:].astype(jnp.float32) for part in parts])
    for e in range(n_experts):
        gate = jnp.sum(jnp.where(lane == lanes_ref[e], gates, 0.0), axis=1, keepdims=True)
        both = jnp.dot(rows_ref[...], w_in[e][...], preferred_element_type=jnp.float32)
        a, b = both[:, :half], both[:, half:]
        hidden_ref[:, e * half : (e + 1) * half] = (a / (1.0 + jnp.exp(-a)) * (b * gate)).astype(
            jnp.bfloat16
        )
    step = width // 2
    for j in range(0, width, step):
        y = jnp.dot(
            hidden_ref[:, :half], w_out[0][:, j : j + step], preferred_element_type=jnp.float32
        )
        for e in range(1, n_experts):
            y = y + jnp.dot(
                hidden_ref[:, e * half : (e + 1) * half],
                w_out[e][:, j : j + step],
                preferred_element_type=jnp.float32,
            )
        each = y.shape[0] // len(outs)
        for p, out in enumerate(outs):
            out[:, j : j + step] = y[p * each : (p + 1) * each].astype(out.dtype)


def experts(parts, lanes, w_in, w_out, dtype, n_outs):
    n_parts, n_experts = len(parts), len(w_in)
    cut, (half, width) = parts[0].shape[0], w_out[0].shape
    count = n_parts * cut
    return pl.pallas_call(
        functools.partial(experts_kernel, n_parts, n_experts),
        out_shape=[pltpu.VMEM((count // n_outs, width), dtype)] * n_outs,
        in_specs=[SMEM_SPEC] + [VMEM_SPEC] * (n_parts + 2 * n_experts),
        out_specs=[VMEM_SPEC] * n_outs,
        scratch_shapes=[
            pltpu.VMEM((count, width), jnp.bfloat16),
            pltpu.VMEM((count, n_experts * half), jnp.bfloat16),
        ],
        compiler_params=params(7),
        cost_estimate=QUICK,
        name="experts",
    )(lanes, *(in_vmem(v) for v in (*parts, *w_in, *w_out)))


def finish_kernel(n_parts, *refs):
    mine, moved, out = refs[:n_parts], refs[n_parts : 2 * n_parts], refs[-1]
    cut = mine[0].shape[0]
    for p in range(n_parts):
        out[p * cut : (p + 1) * cut, :] = (
            mine[p][...] + moved[p][...].astype(jnp.float32)
        ).astype(jnp.bfloat16)


def finish(mine, moved):
    n_parts = len(mine)
    cut, width = mine[0].shape
    return pl.pallas_call(
        functools.partial(finish_kernel, n_parts),
        out_shape=jax.ShapeDtypeStruct((n_parts * cut, width), jnp.bfloat16),
        in_specs=[VMEM_SPEC] * (2 * n_parts),
        out_specs=VMEM_SPEC,
        compiler_params=params(3),
        cost_estimate=QUICK,
        name="finish",
    )(*(in_vmem(v) for v in (*mine, *moved)))


def body(tokens, expert_ids, gate_weights, w_in, w_in_scale, w_out, w_out_scale):
    devices = lax.axis_size("expert")
    chips = devices // CORES
    here = lax.axis_index("expert")
    sibling = here + 1 - 2 * (here % CORES)
    lanes = jnp.stack([here, sibling]).astype(jnp.int32)

    ring = [
        (z * CORES + c, ((z + 1 - 2 * c) % chips) * CORES + c)
        for z in range(chips)
        for c in range(CORES)
    ]

    def hop(value):
        return lax.ppermute(value, "expert", ring)

    def swap(value):
        return lax.ppermute(value, "expert", [(d, d ^ 1) for d in range(devices)])

    def after(values, *earlier):
        return lax.optimization_barrier((values, *earlier))[0]

    raw_in, raw_out = swap(w_in[0]), swap(w_out[0])
    scales = jnp.concatenate([w_in_scale.reshape(-1), w_out_scale.reshape(-1)])
    second = w_in_scale.size
    sib_scales = swap(scales)

    parts = {0: prepare(tokens, expert_ids, gate_weights)}

    def pass_on(s, *earlier):
        parts[s] = [hop(v) for v in after(parts[s - 1], *earlier)]

    pass_on(1)
    own = after((w_in[0], w_out[0]), parts[0])
    own_in, own_out = dequantize(own, scales, (0, second), True)
    pass_on(2, own_out)
    (sib_in,) = dequantize([after(raw_in, parts[1])], sib_scales, (0,))
    (sib_out,) = dequantize([after(raw_out, sib_in)], sib_scales, (second,), kept=(sib_in,))
    pass_on(3, sib_out)
    weights = ([own_in, sib_in], [own_out, sib_out])

    moving, last = None, sib_out
    for s in range(1, chips):
        rows = after(parts[s], last, parts[min(s + 1, chips - 1)])
        n_outs = PIECES if s < chips - 0 else 2 * PIECES
        got = experts(rows, lanes, *weights, jnp.bfloat16 if s == 1 else jnp.float32, n_outs)
        if s == 6:
            mine = experts(after(parts[0], got), lanes, *weights, jnp.float32, PIECES)
            got = after(got, mine)
        if moving is not None:
            if len(moving) < n_outs:
                moving = [half for m in moving for half in jnp.split(m, 2)]
            got = [(m.astype(jnp.float32) + g).astype(jnp.bfloat16) for m, g in zip(moving, got)]
        last = got
        if s + 3 < chips:
            pass_on(s + 3, last)
        moving = [hop(g) for g in got]
    return finish(mine, moving)


def solution(mesh):
    placed = (
        P(("dp", "expert"), None),
        P(("dp", "expert"), None),
        P(("dp", "expert"), None),
        P("expert", None, None),
        P("expert", None, None),
        P("expert", None, None),
        P("expert", None, None),
    )
    return jax.shard_map(
        body, mesh=mesh, in_specs=placed, out_specs=P(("dp", "expert"), None), check_vma=False
    )
```

```python
import functools

import jax
import jax.numpy as jnp
from jax import lax
from jax.experimental import pallas as pl
from jax.experimental.pallas import tpu as pltpu
from jax.sharding import PartitionSpec as P

QB = 128
CORES = 2
LANES = 128
PIECES = 2
MIB = 1024 * 1024
VMEM_SPEC = pl.BlockSpec(memory_space=pltpu.VMEM)
SMEM_SPEC = pl.BlockSpec(memory_space=pltpu.SMEM)
ANY_SPEC = pl.BlockSpec(memory_space=pl.ANY)
QUICK = pl.CostEstimate(flops=1, bytes_accessed=1, transcendentals=0)


def in_hbm(value):
    return pltpu.with_memory_space_constraint(value, pltpu.HBM)


def in_vmem(value):
    return pltpu.with_memory_space_constraint(value, pltpu.VMEM)


def params(mib):
    return pltpu.CompilerParams(vmem_limit_bytes=int(mib * MIB))


def prepare_kernel(tokens_ref, ids_ref, gates_ref, *refs):
    outs, (ids_buf, gates_buf, sems) = refs[:PIECES], refs[PIECES:]
    count, width = tokens_ref.shape
    cut = count // PIECES
    small = [
        pltpu.make_async_copy(ids_ref, ids_buf, sems.at[PIECES]),
        pltpu.make_async_copy(gates_ref, gates_buf, sems.at[PIECES + 1]),
    ]
    large = [
        pltpu.make_async_copy(
            tokens_ref.at[pl.ds(i * cut, cut)], out.at[:, pl.ds(0, width)], sems.at[i]
        )
        for i, out in enumerate(outs)
    ]
    for copy in small + large:
        copy.start()
    for copy in small:
        copy.wait()
    ids, gates = ids_buf[...], gates_buf[...].astype(jnp.float32)
    row = lax.broadcasted_iota(jnp.int32, (LANES, count), 0)
    dense = jnp.zeros((LANES, count), jnp.float32)
    for k in range(ids.shape[0]):
        dense = dense + jnp.where(ids[k : k + 1, :] == row, gates[k : k + 1, :], 0.0)
    dense = dense.T.astype(jnp.bfloat16)
    for i, out in enumerate(outs):
        out[:, width:] = dense[i * cut : (i + 1) * cut]
    for copy in large:
        copy.wait()


def prepare(tokens, expert_ids, gate_weights):
    count, width = tokens.shape
    slots = expert_ids.shape[1]
    return pl.pallas_call(
        prepare_kernel,
        out_shape=[pltpu.VMEM((count // PIECES, width + LANES), jnp.bfloat16)] * PIECES,
        in_specs=[ANY_SPEC] * 3,
        out_specs=[VMEM_SPEC] * PIECES,
        scratch_shapes=[
            pltpu.VMEM((slots, count), jnp.int32),
            pltpu.VMEM((slots, count), jnp.bfloat16),
            pltpu.SemaphoreType.DMA((PIECES + 2,)),
        ],
        compiler_params=params(1),
        cost_estimate=QUICK,
        name="prepare",
    )(in_hbm(tokens), in_hbm(expert_ids.T), in_hbm(gate_weights.T))


def dequantize_kernel(n, turned, via, *refs):
    scales, weights, outs, refs = refs[:n], refs[n : 2 * n], refs[2 * n : 3 * n], refs[3 * n :]
    works, refs = (refs[:n], refs[n:]) if via else (outs, refs)
    arrived, leaving = [], []
    for weight, work in zip(weights, works):
        for i in range(weight.shape[0] // QB):
            at = pl.ds(i * QB, QB)
            arrived.append(
                pltpu.make_async_copy(weight.at[at], work.at[at], refs[0].at[len(arrived)])
            )
            arrived[-1].start()
    done = 0
    for turn, scale, work, out in zip(turned, scales, works, outs):
        rows, cols = work.shape
        for i in range(rows // QB):
            arrived[done].wait()
            for j in range(cols // QB):
                at = slice(i * QB, (i + 1) * QB), slice(j * QB, (j + 1) * QB)
                factor = scale[j, 0, i] if turn else scale[i, 0, j]
                work[at] = (work[at].astype(jnp.float32) * factor).astype(jnp.bfloat16)
            if via:
                at = pl.ds(i * QB, QB)
                leaving.append(pltpu.make_async_copy(work.at[at], out.at[at], refs[1].at[done]))
                leaving[-1].start()
            done += 1
    for copy in leaving:
        copy.wait()


def dequantize(weights, scales, turned, via=False):
    n = len(weights)
    blocks = pltpu.SemaphoreType.DMA((sum(w.shape[0] // QB for w in weights),))
    space = pltpu.HBM if via else pltpu.VMEM
    works = [pltpu.VMEM(w.shape, jnp.bfloat16) for w in weights] if via else []
    return pl.pallas_call(
        functools.partial(dequantize_kernel, n, turned, via),
        out_shape=[space(w.shape, jnp.bfloat16) for w in weights],
        in_specs=[SMEM_SPEC] * n + [ANY_SPEC] * n,
        out_specs=[ANY_SPEC if via else VMEM_SPEC] * n,
        scratch_shapes=[*works, blocks, blocks],
        compiler_params=params(0.5 + sum(w.size for w in weights) * 2 * via / MIB),
        cost_estimate=QUICK,
        name="dequantize",
    )(*(in_hbm(v) for v in (*scales, *weights)))


def experts_kernel(n_parts, n_experts, lanes_ref, *refs):
    parts, refs = refs[:n_parts], refs[n_parts:]
    w_in, refs = refs[:n_experts], refs[n_experts:]
    w_out, refs = refs[:n_experts], refs[n_experts:]
    outs, (rows_ref, hidden_ref) = refs[:-2], refs[-2:]
    half, width = w_out[0].shape
    cut = parts[0].shape[0]
    lane = lax.broadcasted_iota(jnp.int32, (n_parts * cut, LANES), 1)
    for p, part in enumerate(parts):
        rows_ref[p * cut : (p + 1) * cut, :] = part[:, :width]
    gates = jnp.concatenate([part[:, width:].astype(jnp.float32) for part in parts])
    for e in range(n_experts):
        gate = jnp.sum(jnp.where(lane == lanes_ref[e], gates, 0.0), axis=1, keepdims=True)
        both = jnp.dot(rows_ref[...], w_in[e][...], preferred_element_type=jnp.float32)
        a, b = both[:, :half], both[:, half:]
        hidden_ref[:, e * half : (e + 1) * half] = (a / (1.0 + jnp.exp(-a)) * (b * gate)).astype(
            jnp.bfloat16
        )
    step = width // 2
    for j in range(0, width, step):
        y = jnp.dot(
            hidden_ref[:, :half], w_out[0][:, j : j + step], preferred_element_type=jnp.float32
        )
        for e in range(1, n_experts):
            y = y + jnp.dot(
                hidden_ref[:, e * half : (e + 1) * half],
                w_out[e][:, j : j + step],
                preferred_element_type=jnp.float32,
            )
        each = y.shape[0] // len(outs)
        for p, out in enumerate(outs):
            out[:, j : j + step] = y[p * each : (p + 1) * each].astype(out.dtype)


def experts(parts, lanes, w_in, w_out, dtype, n_outs):
    n_parts, n_experts = len(parts), len(w_in)
    cut, (half, width) = parts[0].shape[0], w_out[0].shape
    count = n_parts * cut
    return pl.pallas_call(
        functools.partial(experts_kernel, n_parts, n_experts),
        out_shape=[pltpu.VMEM((count // n_outs, width), dtype)] * n_outs,
        in_specs=[SMEM_SPEC] + [VMEM_SPEC] * (n_parts + 2 * n_experts),
        out_specs=[VMEM_SPEC] * n_outs,
        scratch_shapes=[
            pltpu.VMEM((count, width), jnp.bfloat16),
            pltpu.VMEM((count, n_experts * half), jnp.bfloat16),
        ],
        compiler_params=params(7),
        cost_estimate=QUICK,
        name="experts",
    )(lanes, *(in_vmem(v) for v in (*parts, *w_in, *w_out)))


def finish_kernel(n_parts, *refs):
    mine, moved, out = refs[:n_parts], refs[n_parts : 2 * n_parts], refs[-1]
    cut = mine[0].shape[0]
    for p in range(n_parts):
        out[p * cut : (p + 1) * cut, :] = (
            mine[p][...] + moved[p][...].astype(jnp.float32)
        ).astype(jnp.bfloat16)


def finish(mine, moved):
    n_parts = len(mine)
    cut, width = mine[0].shape
    return pl.pallas_call(
        functools.partial(finish_kernel, n_parts),
        out_shape=jax.ShapeDtypeStruct((n_parts * cut, width), jnp.bfloat16),
        in_specs=[VMEM_SPEC] * (2 * n_parts),
        out_specs=VMEM_SPEC,
        compiler_params=params(3),
        cost_estimate=QUICK,
        name="finish",
    )(*(in_vmem(v) for v in (*mine, *moved)))


def body(tokens, expert_ids, gate_weights, w_in, w_in_scale, w_out, w_out_scale):
    devices = lax.axis_size("expert")
    chips = devices // CORES
    here = lax.axis_index("expert")
    sibling = here + 1 - 2 * (here % CORES)
    lanes = jnp.stack([here, sibling]).astype(jnp.int32)

    ring = [
        (z * CORES + c, ((z + 1 - 2 * c) % chips) * CORES + c)
        for z in range(chips)
        for c in range(CORES)
    ]

    def hop(value):
        return lax.ppermute(value, "expert", ring)

    def swap(value):
        return lax.ppermute(value, "expert", [(d, d ^ 1) for d in range(devices)])

    def after(values, *earlier):
        return lax.optimization_barrier((values, *earlier))[0]

    own_scales = [jnp.transpose(w_in_scale, (2, 0, 1)), jnp.transpose(w_out_scale, (1, 0, 2))]
    sib_scales = [swap(v) for v in own_scales]
    parts = {0: prepare(tokens, expert_ids, gate_weights)}
    raw_in, raw_out = (swap(v) for v in after([w_in[0], w_out[0]], sib_scales, parts[0]))

    def pass_on(s, *earlier):
        parts[s] = [hop(after(v, *earlier)) for v in parts[s - 1]]

    pass_on(1)
    own_in, own_out = dequantize(after([w_in[0], w_out[0]], parts[0]), own_scales, (True, False))
    pass_on(2, own_in)
    sib_in, sib_out = dequantize(
        after([raw_in, raw_out], own_out, parts[1]), sib_scales, (True, False)
    )
    pass_on(3, sib_in)
    weights = ([own_in, sib_in], [own_out, sib_out])

    moving, last = None, sib_out
    for s in range(1, chips):
        n_outs = PIECES if s < chips - 2 else 2 * PIECES
        rows = after(parts[s], last, parts[s + 1][0] if s < 6 else last)
        got = experts(rows, lanes, *weights, jnp.bfloat16 if s == 1 else jnp.float32, n_outs)
        if moving is not None:
            if len(moving) < n_outs:
                moving = [half for m in moving for half in jnp.split(m, 2)]
            got = [(m.astype(jnp.float32) + g).astype(jnp.bfloat16) for m, g in zip(moving, got)]
        last = got
        if s == 7:
            mine = experts(after(parts[0], got), lanes, *weights, jnp.float32, 2 * PIECES)
            last = (got, mine)
        if s + 3 < chips:
            pass_on(s + 3, last)
        moving = [hop(g) for g in got]
    return finish(mine, moving)


def solution(mesh):
    placed = (
        P(("dp", "expert"), None),
        P(("dp", "expert"), None),
        P(("dp", "expert"), None),
        P("expert", None, None),
        P("expert", None, None),
        P("expert", None, None),
        P("expert", None, None),
    )
    return jax.shard_map(
        body, mesh=mesh, in_specs=placed, out_specs=P(("dp", "expert"), None), check_vma=False
    )
```

```python
import functools

import jax
import jax.numpy as jnp
from jax import lax
from jax.experimental import pallas as pl
from jax.experimental.pallas import tpu as pltpu
from jax.sharding import PartitionSpec as P

QB = 128
CORES = 2
LANES = 128
PIECES = 2
MIB = 1024 * 1024
VMEM_SPEC = pl.BlockSpec(memory_space=pltpu.VMEM)
SMEM_SPEC = pl.BlockSpec(memory_space=pltpu.SMEM)
ANY_SPEC = pl.BlockSpec(memory_space=pl.ANY)
QUICK = pl.CostEstimate(flops=1, bytes_accessed=1, transcendentals=0)


def in_hbm(value):
    return pltpu.with_memory_space_constraint(value, pltpu.HBM)


def in_vmem(value):
    return pltpu.with_memory_space_constraint(value, pltpu.VMEM)


def params(mib):
    return pltpu.CompilerParams(vmem_limit_bytes=int(mib * MIB))


def prepare_kernel(tokens_ref, ids_ref, gates_ref, *refs):
    outs, (ids_buf, gates_buf, sems) = refs[:PIECES], refs[PIECES:]
    count, width = tokens_ref.shape
    cut = count // PIECES
    small = [
        pltpu.make_async_copy(ids_ref, ids_buf, sems.at[PIECES]),
        pltpu.make_async_copy(gates_ref, gates_buf, sems.at[PIECES + 1]),
    ]
    large = [
        pltpu.make_async_copy(
            tokens_ref.at[pl.ds(i * cut, cut)], out.at[:, pl.ds(0, width)], sems.at[i]
        )
        for i, out in enumerate(outs)
    ]
    for copy in small + large:
        copy.start()
    for copy in small:
        copy.wait()
    ids, gates = ids_buf[...], gates_buf[...].astype(jnp.float32)
    row = lax.broadcasted_iota(jnp.int32, (LANES, count), 0)
    dense = jnp.zeros((LANES, count), jnp.float32)
    for k in range(ids.shape[0]):
        dense = dense + jnp.where(ids[k : k + 1, :] == row, gates[k : k + 1, :], 0.0)
    dense = dense.T.astype(jnp.bfloat16)
    for i, out in enumerate(outs):
        out[:, width:] = dense[i * cut : (i + 1) * cut]
    for copy in large:
        copy.wait()


def prepare(tokens, expert_ids, gate_weights):
    count, width = tokens.shape
    slots = expert_ids.shape[1]
    return pl.pallas_call(
        prepare_kernel,
        out_shape=[pltpu.VMEM((count // PIECES, width + LANES), jnp.bfloat16)] * PIECES,
        in_specs=[ANY_SPEC] * 3,
        out_specs=[VMEM_SPEC] * PIECES,
        scratch_shapes=[
            pltpu.VMEM((slots, count), jnp.int32),
            pltpu.VMEM((slots, count), jnp.bfloat16),
            pltpu.SemaphoreType.DMA((PIECES + 2,)),
        ],
        compiler_params=params(1),
        cost_estimate=QUICK,
        name="prepare",
    )(in_hbm(tokens), in_hbm(expert_ids.T), in_hbm(gate_weights.T))


def dequantize_kernel(n, turned, via, *refs):
    scales, weights, outs, refs = refs[:n], refs[n : 2 * n], refs[2 * n : 3 * n], refs[3 * n :]
    works, refs = (refs[:n], refs[n:]) if via else (outs, refs)
    arrived, leaving = [], []
    for weight, work in zip(weights, works):
        for i in range(weight.shape[0] // QB):
            at = pl.ds(i * QB, QB)
            arrived.append(
                pltpu.make_async_copy(weight.at[at], work.at[at], refs[0].at[len(arrived)])
            )
            arrived[-1].start()
    done = 0
    for turn, scale, work, out in zip(turned, scales, works, outs):
        rows, cols = work.shape
        for i in range(rows // QB):
            arrived[done].wait()
            for j in range(cols // QB):
                at = slice(i * QB, (i + 1) * QB), slice(j * QB, (j + 1) * QB)
                factor = scale[j, 0, i] if turn else scale[i, 0, j]
                work[at] = (work[at].astype(jnp.float32) * factor).astype(jnp.bfloat16)
            if via:
                at = pl.ds(i * QB, QB)
                leaving.append(pltpu.make_async_copy(work.at[at], out.at[at], refs[1].at[done]))
                leaving[-1].start()
            done += 1
    for copy in leaving:
        copy.wait()


def dequantize(weights, scales, turned, via=False):
    n = len(weights)
    blocks = pltpu.SemaphoreType.DMA((sum(w.shape[0] // QB for w in weights),))
    space = pltpu.HBM if via else pltpu.VMEM
    works = [pltpu.VMEM(w.shape, jnp.bfloat16) for w in weights] if via else []
    return pl.pallas_call(
        functools.partial(dequantize_kernel, n, turned, via),
        out_shape=[space(w.shape, jnp.bfloat16) for w in weights],
        in_specs=[SMEM_SPEC] * n + [ANY_SPEC] * n,
        out_specs=[ANY_SPEC if via else VMEM_SPEC] * n,
        scratch_shapes=[*works, blocks, blocks],
        compiler_params=params(0.5 + sum(w.size for w in weights) * 2 * via / MIB),
        cost_estimate=QUICK,
        name="dequantize",
    )(*(in_hbm(v) for v in (*scales, *weights)))


def experts_kernel(n_parts, n_experts, lanes_ref, *refs):
    parts, refs = refs[:n_parts], refs[n_parts:]
    w_in, refs = refs[:n_experts], refs[n_experts:]
    w_out, refs = refs[:n_experts], refs[n_experts:]
    outs, (rows_ref, hidden_ref) = refs[:-2], refs[-2:]
    half, width = w_out[0].shape
    cut = parts[0].shape[0]
    lane = lax.broadcasted_iota(jnp.int32, (n_parts * cut, LANES), 1)
    for p, part in enumerate(parts):
        rows_ref[p * cut : (p + 1) * cut, :] = part[:, :width]
    gates = jnp.concatenate([part[:, width:].astype(jnp.float32) for part in parts])
    for e in range(n_experts):
        gate = jnp.sum(jnp.where(lane == lanes_ref[e], gates, 0.0), axis=1, keepdims=True)
        both = jnp.dot(rows_ref[...], w_in[e][...], preferred_element_type=jnp.float32)
        a, b = both[:, :half], both[:, half:]
        hidden_ref[:, e * half : (e + 1) * half] = (a / (1.0 + jnp.exp(-a)) * (b * gate)).astype(
            jnp.bfloat16
        )
    step = width // 2
    for j in range(0, width, step):
        y = jnp.dot(
            hidden_ref[:, :half], w_out[0][:, j : j + step], preferred_element_type=jnp.float32
        )
        for e in range(1, n_experts):
            y = y + jnp.dot(
                hidden_ref[:, e * half : (e + 1) * half],
                w_out[e][:, j : j + step],
                preferred_element_type=jnp.float32,
            )
        each = y.shape[0] // len(outs)
        for p, out in enumerate(outs):
            out[:, j : j + step] = y[p * each : (p + 1) * each].astype(out.dtype)


def experts(parts, lanes, w_in, w_out, dtype, n_outs):
    n_parts, n_experts = len(parts), len(w_in)
    cut, (half, width) = parts[0].shape[0], w_out[0].shape
    count = n_parts * cut
    return pl.pallas_call(
        functools.partial(experts_kernel, n_parts, n_experts),
        out_shape=[pltpu.VMEM((count // n_outs, width), dtype)] * n_outs,
        in_specs=[SMEM_SPEC] + [VMEM_SPEC] * (n_parts + 2 * n_experts),
        out_specs=[VMEM_SPEC] * n_outs,
        scratch_shapes=[
            pltpu.VMEM((count, width), jnp.bfloat16),
            pltpu.VMEM((count, n_experts * half), jnp.bfloat16),
        ],
        compiler_params=params(7),
        cost_estimate=QUICK,
        name="experts",
    )(lanes, *(in_vmem(v) for v in (*parts, *w_in, *w_out)))


def finish_kernel(n_parts, *refs):
    mine, moved, out = refs[:n_parts], refs[n_parts : 2 * n_parts], refs[-1]
    cut = mine[0].shape[0]
    for p in range(n_parts):
        out[p * cut : (p + 1) * cut, :] = (
            mine[p][...] + moved[p][...].astype(jnp.float32)
        ).astype(jnp.bfloat16)


def finish(mine, moved):
    n_parts = len(mine)
    cut, width = mine[0].shape
    return pl.pallas_call(
        functools.partial(finish_kernel, n_parts),
        out_shape=jax.ShapeDtypeStruct((n_parts * cut, width), jnp.bfloat16),
        in_specs=[VMEM_SPEC] * (2 * n_parts),
        out_specs=VMEM_SPEC,
        compiler_params=params(3),
        cost_estimate=QUICK,
        name="finish",
    )(*(in_vmem(v) for v in (*mine, *moved)))


def body(tokens, expert_ids, gate_weights, w_in, w_in_scale, w_out, w_out_scale):
    devices = lax.axis_size("expert")
    chips = devices // CORES
    here = lax.axis_index("expert")
    sibling = here + 1 - 2 * (here % CORES)
    lanes = jnp.stack([here, sibling]).astype(jnp.int32)

    ring = [
        (z * CORES + c, ((z + 1 - 2 * c) % chips) * CORES + c)
        for z in range(chips)
        for c in range(CORES)
    ]

    def hop(value):
        return lax.ppermute(value, "expert", ring)

    def swap(value):
        return lax.ppermute(value, "expert", [(d, d ^ 1) for d in range(devices)])

    def after(values, *earlier):
        return lax.optimization_barrier((values, *earlier))[0]

    own_scales = [jnp.transpose(w_in_scale, (2, 0, 1)), jnp.transpose(w_out_scale, (1, 0, 2))]
    sib_scales = [swap(v) for v in own_scales]
    parts = {0: prepare(tokens, expert_ids, gate_weights)}
    raw_in, raw_out = (swap(v) for v in after([w_in[0], w_out[0]], sib_scales, parts[0]))

    def pass_on(s, *earlier):
        parts[s] = [hop(after(v, *earlier)) for v in parts[s - 1]]

    pass_on(1)
    own_in, own_out = dequantize(after([w_in[0], w_out[0]], parts[0]), own_scales, (True, False))
    pass_on(2, own_in)
    sib_in, sib_out = dequantize(
        after([raw_in, raw_out], own_out, parts[1]), sib_scales, (True, False)
    )
    pass_on(3, sib_in)
    weights = ([own_in, sib_in], [own_out, sib_out])

    moving, last = None, sib_out
    for s in range(1, chips):
        n_outs = PIECES if s < chips - 1 else 2 * PIECES
        rows = after(parts[s], last, parts[s + 1][0] if s < 6 else last)
        got = experts(rows, lanes, *weights, jnp.bfloat16 if s == 1 else jnp.float32, n_outs)
        if moving is not None:
            if len(moving) < n_outs:
                moving = [half for m in moving for half in jnp.split(m, 2)]
            got = [(m.astype(jnp.float32) + g).astype(jnp.bfloat16) for m, g in zip(moving, got)]
        last = got
        if s == 7:
            mine = experts(after(parts[0], got), lanes, *weights, jnp.float32, 2 * PIECES)
            last = (got, mine)
        if s + 3 < chips:
            pass_on(s + 3, last)
        moving = [hop(g) for g in got]
    return finish(mine, moving)


def solution(mesh):
    placed = (
        P(("dp", "expert"), None),
        P(("dp", "expert"), None),
        P(("dp", "expert"), None),
        P("expert", None, None),
        P("expert", None, None),
        P("expert", None, None),
        P("expert", None, None),
    )
    return jax.shard_map(
        body, mesh=mesh, in_specs=placed, out_specs=P(("dp", "expert"), None), check_vma=False
    )
```
